256 devices in a mesh: dp: 16 (over z, x_hi), replica: 16 (over x_lo, y, core).
Axes of the slice: x: 4 (x_hi: 2, x_lo: 2; x = x_hi * 2 + x_lo), y: 4, z: 8, core: 2. Of those that a mesh axis runs over, the one named last changes fastest.
Arguments:
- images: float32 [16, 6144, 1152], P('replica', 'dp'), may hold values from -6 to 6
- texts: float32 [16, 6144, 1152], P('replica', 'dp'), may hold values from -6 to 6
- pairs: int32 [16, 16, 384], P('replica', 'dp'), may hold values from 0 to 383, each once within a row
- log_temp: float32 [1], replicated, may hold values from -3 to -2
- bias: float32 [1], replicated, may hold values from -4 to -1
Outputs:
- grad_images: float32 [16, 6144, 1152], P('replica', 'dp')
- grad_texts: float32 [16, 6144, 1152], P('replica', 'dp')
- stats: float32 [3], replicated
The draws below stay inside these ranges and needn't reach their ends.
Inputs may be any that keep to these rules, and one draw needn't show every extreme that they name: `pairs`: each image's paired text lies in the image's own block; within a block every position is paired once.
All inputs are finite; a program needn't handle non-finite values.
Results may differ from the reference program's by a relative error of at most 0.00018.
Values sent between devices are 32-bit elements; how exact they have to be, the bound alone decides.
No kernel may reach another device: no remote copies, remote signals or barrier semaphores. Data moves between devices by JAX's collectives and lax.ppermute only.
A program may use at most 128 MiB of HBM per device.

```python
import jax
import jax.numpy as jnp
from jax import lax

D = 1152
TOK_DEV = 384
HOPS = 8
TOKENS = 6144
GROUPS = 16
N_DP = 16
N_REPLICA = 16


def steps_of(key, dims, pieces, least, top_value):
    loudness = 1.0
    for dim, parts in pieces:
        heights = jax.random.uniform(jax.random.fold_in(jax.random.fold_in(key, 6), dim), (parts,), jnp.float32, least / len(pieces), top_value / len(pieces))
        loudness = loudness * jnp.repeat(jnp.exp(heights), dims[dim] // parts).reshape((-1,) + (1,) * (len(dims) - 1 - dim))
    return loudness


def noise(stream_key, extent, spread, limit, split=(), kind=jnp.bfloat16):
    result = spread * jax.random.normal(stream_key, extent, jnp.float32)
    if split:
        result = result * steps_of(stream_key, extent, split, -0.22, 0.18)
    return jnp.clip(result, -limit, limit).astype(kind)


def setup_inputs(seed: int = 0) -> dict:
    key_list = jax.random.split(jax.random.key(seed), 6)
    images = noise(key_list[0], (GROUPS, TOKENS, D), 1.0, 6.0, ((0, 16), (1, 16)), jnp.float32)
    texts = noise(key_list[1], (GROUPS, TOKENS, D), 1.0, 6.0, ((0, 16), (1, 16)), jnp.float32)
    pairs = jax.vmap(lambda own: jax.random.permutation(own, TOK_DEV))(jax.random.split(key_list[2], GROUPS * N_DP)).reshape((GROUPS, N_DP, TOK_DEV)).astype(jnp.int32)
    log_temp = jnp.clip(jax.random.uniform(key_list[3], (1,), jnp.float32, -3.0, -2.0), -3.0, -2.0)
    bias = jnp.clip(jax.random.uniform(key_list[4], (1,), jnp.float32, -4.0, -1.0), -4.0, -1.0)
    return {"images": images, "texts": texts, "pairs": pairs, "log_temp": log_temp, "bias": bias}


def reference(images, texts, pairs, log_temp, bias):
    scale = jnp.exp(log_temp[0])
    shift_b = bias[0]
    x = images.reshape(N_REPLICA, N_DP, TOK_DEV, D)
    y = texts.reshape(N_REPLICA, N_DP, TOK_DEV, D)
    columns = jnp.arange(TOK_DEV, dtype=jnp.int32)
    positive = (columns[None, None, None, :] == pairs[..., None].astype(jnp.int32)).astype(jnp.float32)
    grad_x = jnp.zeros_like(x)
    grad_y = jnp.zeros_like(y)
    loss_sum = jnp.float32(0.0)
    temp_sum = jnp.float32(0.0)
    bias_sum = jnp.float32(0.0)
    for hop in range(HOPS):
        moved = jnp.roll(y, hop, axis=1)
        scores = scale * jnp.einsum("gbid,gbjd->gbij", x, moved, precision=lax.Precision.HIGHEST) + shift_b
        marked = positive if hop == 0 else jnp.zeros_like(scores)
        coef = jax.nn.sigmoid(scores) - marked
        loss_sum = loss_sum + jnp.sum(jax.nn.softplus(scores) - marked * scores)
        temp_sum = temp_sum + jnp.sum(coef * (scores - shift_b))
        bias_sum = bias_sum + jnp.sum(coef)
        grad_x = grad_x + scale * jnp.einsum("gbij,gbjd->gbid", coef, moved, precision=lax.Precision.HIGHEST)
        partial_y = scale * jnp.einsum("gbij,gbid->gbjd", coef, x, precision=lax.Precision.HIGHEST)
        grad_y = grad_y + jnp.roll(partial_y, -hop, axis=1)
    count = float(HOPS * N_REPLICA * N_DP * TOK_DEV * TOK_DEV)
    stats = jnp.stack([loss_sum, temp_sum, bias_sum]) / count
    return grad_x.reshape(images.shape), grad_y.reshape(texts.shape), stats
```

```python
import functools

import jax
import jax.numpy as jnp
from jax import lax
from jax.experimental import pallas as pl
from jax.experimental.pallas import tpu as pltpu
from jax.sharding import PartitionSpec as P

HOPS = 8
AXES = ("dp", "replica")
COLS = 2
MIB = 1024 * 1024
FLOPS_PER_US = 1.15e9

WHOLE = pl.BlockSpec(memory_space=pltpu.VMEM)
ANYWHERE = pl.BlockSpec(memory_space=pl.ANY)
SCALARS = pl.BlockSpec(memory_space=pltpu.SMEM)


ORDER = (
    ((0,), (0,)),
    ((1,), (0,)),
    ((0, 1), (1,)),
    ((0, 1), (2,)),
    ((0, 1), (3,)),
)


def f32(*shape):
    return jax.ShapeDtypeStruct(shape, jnp.float32)


def cost(micros):
    return pl.CostEstimate(
        flops=int(micros * FLOPS_PER_US), bytes_accessed=1024, transcendentals=0
    )


def limits(size=12):
    return pltpu.CompilerParams(vmem_limit_bytes=size * MIB)


def routes(size, replicas, to):
    levels = size // COLS
    pairs = []
    for level in range(levels):
        for col in range(COLS):
            for rep in range(replicas):
                new_level, new_col = to(level, col, rep % 2)
                source = (level * COLS + col) * replicas + rep
                target = ((new_level % levels) * COLS + new_col) * replicas + rep
                pairs.append((source, target))
    return pairs


def ahead(core):
    return 1 - 2 * core


def exchange(value, bit, total):
    return value + lax.ppermute(value, AXES, [(i, i ^ bit) for i in range(total)])


def split(value):
    high = value.astype(jnp.bfloat16)
    low = (value - high.astype(jnp.float32)).astype(jnp.bfloat16)
    return high, low


def dot3(a, b, dims):
    (i,), (j,) = dims
    left = jnp.concatenate([a[0], a[0], a[1]], axis=i)
    right = jnp.concatenate([b[0], b[1], b[0]], axis=j)
    return lax.dot_general(left, right, (dims, ((), ())), preferred_element_type=jnp.float32)


def stack(values, axis=0):
    return jnp.concatenate(values, axis=axis) if len(values) > 1 else values[0]


def hold_kernel(value, token, out):
    del value, token, out


def hold(value, token):
    return pl.pallas_call(
        hold_kernel,
        out_shape=f32(*value.shape),
        in_specs=[ANYWHERE] * 2,
        out_specs=ANYWHERE,
        input_output_aliases={0: 0},
        compiler_params=limits(),
        cost_estimate=cost(0.05),
    )(value, token)


def unit_kernel(first, counts, numbers, partner, before, *refs):
    residents, hops, with_earlier, with_gathered, pieces = counts
    taken = 0

    def take(count):
        nonlocal taken
        taken += count
        return refs[taken - count : taken]

    held, blocks = take(residents), take(hops)
    earlier, gathered = take(with_earlier), take(with_gathered)
    outs, grads, (after,) = take(pieces), take(hops), take(1)
    scale, shift_b = numbers[0], numbers[1]
    rows = held[0].shape[0]
    held_parts = split(stack([ref[...] for ref in held]))
    coefs, parts = [], []
    for i in range(3):
        after[i : i + 1, :] = before[i : i + 1, :]
    for hop in range(hops):
        block_parts = split(blocks[hop][...])
        product = scale * dot3(block_parts, held_parts, ((1,), (1,)))
        scores = product + shift_b
        small = jnp.exp(-jnp.abs(scores))
        share = 1.0 / (1.0 + small)
        coef = jnp.where(scores >= 0, share, small * share)
        loss = jnp.maximum(scores, 0.0) + jnp.log1p(small)
        if first:
            here = lax.broadcasted_iota(jnp.int32, scores.shape, 0) == partner[...]
            coef = coef - here.astype(jnp.float32)
            loss = loss - jnp.where(here, scores, 0.0)
        for i, values in enumerate((loss, coef * product, coef)):
            column_sums = jnp.sum(values, axis=0, keepdims=True)
            for n in range(residents):
                after[i : i + 1, :] += column_sums[:, n * rows : (n + 1) * rows]
        coef_parts = split(scale * coef)
        total = dot3(coef_parts, held_parts, ((1,), (0,)))
        grads[hop][...] = earlier[hop][...] + total if with_earlier else total
        coefs.append(coef_parts)
        parts.append(block_parts)
    total = dot3(
        tuple(stack([value[n] for value in coefs]) for n in range(2)),
        tuple(stack([value[n] for value in parts]) for n in range(2)),
        ((0,), (0,)),
    )
    place = 0
    for i, out in enumerate(outs):
        term = total[place : place + out.shape[0]]
        if with_gathered:
            which, start = place // rows, place % rows
            term = gathered[which][start : start + out.shape[0], :] + term
        out[...] = term
        place += out.shape[0]


def unit(first, numbers, partner, before, blocks, held, earlier, gathered, heights):
    width = held[0].shape[1]
    operands = [partner, before, *held, *blocks, *earlier, *gathered]
    counts = (len(held), len(blocks), len(earlier), len(gathered), len(heights))
    outs = pl.pallas_call(
        functools.partial(unit_kernel, first, counts),
        out_shape=[f32(height, width) for height in heights]
        + [f32(*block.shape) for block in blocks]
        + [f32(*before.shape)],
        in_specs=[SCALARS] + [WHOLE] * len(operands),
        out_specs=[WHOLE] * (len(heights) + len(blocks) + 1),
        compiler_params=limits(14 + 8 * (len(held) * len(blocks) - 1)),
        cost_estimate=cost(7.0 * len(held) * len(blocks)),
    )(numbers, *operands)
    return outs[: len(heights)], outs[len(heights) : -1], outs[-1]


def add_kernel(left, right, *refs):
    refs[-1][...] = left[...] + right[...]


def add(left, right, *tokens):
    return pl.pallas_call(
        add_kernel,
        out_shape=f32(*left.shape),
        in_specs=[WHOLE] * 2 + [ANYWHERE] * len(tokens),
        out_specs=WHOLE,
        compiler_params=limits(),
        cost_estimate=cost(0.3),
    )(left, right, *tokens)


def place_kernel(start, chosen, left, right, token, *refs):
    out_x, out_y, total, sem = refs[-4:]
    rows = pl.ds(start, total.shape[0])
    total[...] = left[...] + (right[...] if right.shape == total.shape else right[rows, :])
    to_x = pltpu.make_async_copy(total, out_x.at[rows], sem)
    to_y = pltpu.make_async_copy(total, out_y.at[rows], sem)

    @pl.when(chosen[0] == 0)
    def _():
        to_x.start()
        to_x.wait()

    @pl.when(chosen[0] != 0)
    def _():
        to_y.start()
        to_y.wait()


def place(start, chosen, left, right, token, rows, outs=()):
    part, width = left.shape
    return pl.pallas_call(
        functools.partial(place_kernel, start),
        out_shape=[f32(rows, width)] * 2,
        in_specs=[SCALARS, WHOLE, WHOLE, WHOLE] + [ANYWHERE] * len(outs),
        out_specs=[ANYWHERE] * 2,
        scratch_shapes=[pltpu.VMEM((part, width), jnp.float32), pltpu.SemaphoreType.DMA],
        input_output_aliases={4: 0, 5: 1} if outs else {},
        compiler_params=limits(),
        cost_estimate=cost(1.0),
    )(chosen, left, right, token, *outs)


def on_device(images, texts, pairs, log_temp, bias):
    x_rows = images[0]
    y_rows = texts[0]
    rows = x_rows.shape[0]
    half = rows // 2
    size = lax.axis_size("dp")
    replicas = lax.axis_size("replica")
    numbers = jnp.concatenate([jnp.exp(log_temp), bias])
    core = lax.axis_index("replica") % 2
    swapped = core == 1
    moving_images = jnp.where(swapped, 1, 0).astype(jnp.int32).reshape(1)

    def send(value, to):
        return lax.ppermute(value, AXES, routes(size, replicas, to))

    def onward(value):
        return send(value, lambda z, c, k: (z + ahead(k), c))

    def back(value):
        return send(value, lambda z, c, k: (z - ahead(k), c))

    def across(value):
        return send(value, lambda z, c, k: (z, 1 - c))

    visits = [jnp.where(swapped, x_rows, y_rows)]
    held_b = jnp.where(swapped, y_rows[half:], x_rows[half:])
    held_a = jnp.where(swapped, y_rows[:half], x_rows[:half])
    held = jnp.concatenate([held_a, held_b], axis=0)
    for hop in range(3):
        visits.append(onward(visits[-1]))

    own = pairs[0]
    index = jnp.arange(rows, dtype=jnp.int32)
    inverse = jnp.sum(jnp.where(own == index[:, None], index[None, :], 0), axis=1)
    partner = jnp.where(swapped, inverse[None, :], own)

    sums = jnp.zeros((3, rows), jnp.float32)
    partial = {}
    gathered = {}
    residents = [held, None]
    for step, (which, hops) in enumerate(ORDER):
        if step == 1:
            next_a = send(across(held_a), lambda z, c, k: (z - ahead(k) * (c != k), c))
            next_b = send(held_b, lambda z, c, k: (z - ahead(k) * (c == k), c))
            next_b = across(next_b)
            residents[1] = jnp.concatenate([next_a, next_b], axis=0)
        last = step == len(ORDER) - 1
        outs, terms, sums = unit(
            step == 0,
            numbers,
            partner,
            sums,
            [visits[hop] for hop in hops],
            [residents[n] for n in which],
            [partial[hop] for hop in hops if hop in partial],
            [gathered[n] for n in which if n in gathered],
            [rows, half, half] if last else [rows] * len(which),
        )
        gathered.update(zip(which, outs))
        partial.update(zip(hops, terms))

    grad_own, ret_a, ret_b = outs

    stats = jnp.sum(sums, axis=1)

    def gather(bits, stats):
        for bit in bits:
            stats = exchange(stats, bit, size * replicas)
        return stats

    bits = [1 << n for n in range((size * replicas).bit_length() - 1)]
    column = [replicas // 2, replicas]
    levels = [bit for bit in bits if bit > replicas]
    inner = [bit for bit in bits if bit < replicas // 2]
    up_a = send(ret_a, lambda z, c, k: (z + ahead(k) * (c != k), c))
    over_b = across(ret_b)
    stats = gather(inner + levels[:1], stats)
    total = add(back(partial[3]), partial[2], stats, up_a, over_b)
    home_a = across(up_a)
    home_b = send(over_b, lambda z, c, k: (z + ahead(k) * (c == k), c))
    stats = gather(levels[1:2], stats)
    total = add(back(total), partial[1], stats, home_a, home_b)
    total = back(total)
    stats = gather(levels[2:] + column, stats)
    held_images = 1 - moving_images
    outs = place(0, held_images, home_a, grad_own, numbers, rows)
    outs = place(half, held_images, home_b, grad_own, numbers, rows, outs)
    grad_y, grad_x = place(0, moving_images, total, partial[0], numbers, rows, outs)
    count = float(HOPS * rows * rows * size * replicas)
    stats = stats / count
    return (grad_x[None], grad_y[None], stats)


def solution(mesh):
    placed = (
        P("replica", "dp", None),
        P("replica", "dp", None),
        P("replica", "dp", None),
        P(),
        P(),
    )
    return jax.shard_map(
        on_device,
        mesh=mesh,
        in_specs=placed,
        out_specs=(P("replica", "dp", None), P("replica", "dp", None), P()),
        check_vma=False,
    )
```

```python
import functools

import jax
import jax.numpy as jnp
from jax import lax
from jax.experimental import pallas as pl
from jax.experimental.pallas import tpu as pltpu
from jax.sharding import PartitionSpec as P

HOPS = 8
AXES = ("dp", "replica")
COLS = 2
PARTS = 3
MIB = 1024 * 1024
FLOPS_PER_US = 1.15e9

WHOLE = pl.BlockSpec(memory_space=pltpu.VMEM)
ANYWHERE = pl.BlockSpec(memory_space=pl.ANY)
SCALARS = pl.BlockSpec(memory_space=pltpu.SMEM)


ORDER = (
    ((0,), (0,)),
    ((1,), (0,)),
    ((0, 1), (1,)),
    ((0, 1), (2,)),
    ((0, 1), (3,)),
)


def f32(*shape):
    return jax.ShapeDtypeStruct(shape, jnp.float32)


def cost(micros):
    return pl.CostEstimate(
        flops=int(micros * FLOPS_PER_US), bytes_accessed=1024, transcendentals=0
    )


def limits(size=12):
    return pltpu.CompilerParams(vmem_limit_bytes=size * MIB)


def routes(size, replicas, to):
    levels = size // COLS
    pairs = []
    for level in range(levels):
        for col in range(COLS):
            for rep in range(replicas):
                new_level, new_col = to(level, col, rep % 2)
                source = (level * COLS + col) * replicas + rep
                target = ((new_level % levels) * COLS + new_col) * replicas + rep
                pairs.append((source, target))
    return pairs


def ahead(core):
    return 1 - 2 * core


def exchange(value, bit, total):
    return value + lax.ppermute(value, AXES, [(i, i ^ bit) for i in range(total)])


def split(value):
    high = value.astype(jnp.bfloat16)
    low = (value - high.astype(jnp.float32)).astype(jnp.bfloat16)
    return high, low


def dot3(a, b, dims):
    (i,), (j,) = dims
    left = jnp.concatenate([a[0], a[0], a[1]], axis=i)
    right = jnp.concatenate([b[0], b[1], b[0]], axis=j)
    return lax.dot_general(left, right, (dims, ((), ())), preferred_element_type=jnp.float32)


def stack(values, axis=0):
    return jnp.concatenate(values, axis=axis) if len(values) > 1 else values[0]


def hold_kernel(value, token, out):
    del value, token, out


def hold(value, token):
    return pl.pallas_call(
        hold_kernel,
        out_shape=f32(*value.shape),
        in_specs=[ANYWHERE] * 2,
        out_specs=ANYWHERE,
        input_output_aliases={0: 0},
        compiler_params=limits(),
        cost_estimate=cost(0.05),
    )(value, token)


def unit_kernel(first, later, counts, numbers, partner, before, *refs):
    residents, hops, with_earlier, with_gathered, pieces = counts
    taken = 0

    def take(count):
        nonlocal taken
        taken += count
        return refs[taken - count : taken]

    held, blocks = take(residents), take(hops)
    earlier, gathered = take(with_earlier), take(with_gathered)
    outs, grads, (after,) = take(pieces), take(hops), take(1)
    scale, shift_b = numbers[0], numbers[1]
    rows = held[0].shape[0]
    held_parts = split(stack([ref[...] for ref in held]))
    coefs, parts = [], []
    for i in range(3):
        after[i : i + 1, :] = before[i : i + 1, :]
    for hop in range(hops):
        block_parts = split(blocks[hop][...])
        product = scale * dot3(block_parts, held_parts, ((1,), (1,)))
        scores = product + shift_b
        small = jnp.exp(-jnp.abs(scores))
        share = 1.0 / (1.0 + small)
        coef = jnp.where(scores >= 0, share, small * share)
        loss = jnp.maximum(scores, 0.0) + jnp.log1p(small)
        if first:
            here = lax.broadcasted_iota(jnp.int32, scores.shape, 0) == partner[...]
            coef = coef - here.astype(jnp.float32)
            loss = loss - jnp.where(here, scores, 0.0)
        for i, values in enumerate((loss, coef * product, coef)):
            column_sums = jnp.sum(values, axis=0, keepdims=True)
            for n in range(residents):
                after[i : i + 1, :] += column_sums[:, n * rows : (n + 1) * rows]
        coef_parts = split(scale * coef)
        total = dot3(coef_parts, held_parts, ((1,), (0,)))
        grads[hop][...] = earlier[hop][...] + total if with_earlier else total
        coefs.append(coef_parts)
        parts.append(block_parts)
    if later:
        for n in range(2):
            outs[n][...] = coefs[0][n]
        return
    total = dot3(
        tuple(stack([value[n] for value in coefs]) for n in range(2)),
        tuple(stack([value[n] for value in parts]) for n in range(2)),
        ((0,), (0,)),
    )
    for i, out in enumerate(outs):
        term = total[i * rows : (i + 1) * rows]
        out[...] = gathered[i][...] + term if with_gathered else term


def unit(first, later, numbers, partner, before, blocks, held, earlier, gathered):
    if later:
        count = sum(value.shape[0] for value in held)
        first_shapes = [jax.ShapeDtypeStruct((blocks[0].shape[0], count), jnp.bfloat16)] * 2
        gathered = []
    else:
        first_shapes = [f32(*value.shape) for value in held]
    operands = [partner, before, *held, *blocks, *earlier, *gathered]
    counts = (len(held), len(blocks), len(earlier), len(gathered), len(first_shapes))
    outs = pl.pallas_call(
        functools.partial(unit_kernel, first, later, counts),
        out_shape=first_shapes
        + [f32(*block.shape) for block in blocks]
        + [f32(*before.shape)],
        in_specs=[SCALARS] + [WHOLE] * len(operands),
        out_specs=[WHOLE] * (len(first_shapes) + len(blocks) + 1),
        compiler_params=limits(14 + 8 * (len(held) * len(blocks) - 1)),
        cost_estimate=cost(7.0 * len(held) * len(blocks)),
    )(numbers, *operands)
    return outs[: len(first_shapes)], outs[len(first_shapes) : -1], outs[-1]


def rest_kernel(pieces, high, low, block, *refs):
    block_parts = split(block[...])
    for (column, start, count), sofar, out in zip(pieces, refs[: len(pieces)], refs[len(pieces) :]):
        place = pl.ds(column, count)
        term = dot3((high[:, place], low[:, place]), block_parts, ((0,), (0,)))
        out[...] = sofar[start : start + count, :] + term


def rest(high, low, block, sofar, pieces):
    width = block.shape[1]
    return pl.pallas_call(
        functools.partial(rest_kernel, pieces),
        out_shape=[f32(count, width) for _, _, count in pieces],
        in_specs=[WHOLE] * (3 + len(pieces)),
        out_specs=[WHOLE] * len(pieces),
        compiler_params=limits(16),
        cost_estimate=cost(0.007 * sum(count for _, _, count in pieces)),
    )(high, low, block, *sofar)


def add_kernel(left, right, *refs):
    refs[-1][...] = left[...] + right[...]


def add(left, right, *tokens):
    return pl.pallas_call(
        add_kernel,
        out_shape=f32(*left.shape),
        in_specs=[WHOLE] * 2 + [ANYWHERE] * len(tokens),
        out_specs=WHOLE,
        compiler_params=limits(),
        cost_estimate=cost(0.3),
    )(left, right, *tokens)


def place_kernel(start, chosen, left, right, token, *refs):
    out_x, out_y, total, sem = refs[-4:]
    height = total.shape[0] // PARTS

    def copies(out, i):
        rows = pl.ds(i * height, height)
        return pltpu.make_async_copy(total.at[rows], out.at[pl.ds(start + i * height, height)], sem.at[i])

    for i in range(PARTS):
        rows = pl.ds(i * height, height)
        more = right[rows, :] if right.shape == total.shape else right[pl.ds(start + i * height, height), :]
        total[rows, :] = left[rows, :] + more

        @pl.when(chosen[0] == 0)
        def _():
            copies(out_x, i).start()

        @pl.when(chosen[0] != 0)
        def _():
            copies(out_y, i).start()

    for i in range(PARTS):

        @pl.when(chosen[0] == 0)
        def _():
            copies(out_x, i).wait()

        @pl.when(chosen[0] != 0)
        def _():
            copies(out_y, i).wait()


def place(start, chosen, left, right, token, rows, outs=()):
    part, width = left.shape
    return pl.pallas_call(
        functools.partial(place_kernel, start),
        out_shape=[f32(rows, width)] * 2,
        in_specs=[SCALARS, WHOLE, WHOLE, WHOLE] + [ANYWHERE] * len(outs),
        out_specs=[ANYWHERE] * 2,
        scratch_shapes=[pltpu.VMEM((part, width), jnp.float32), pltpu.SemaphoreType.DMA((PARTS,))],
        input_output_aliases={4: 0, 5: 1} if outs else {},
        compiler_params=limits(),
        cost_estimate=cost(1.0),
    )(chosen, left, right, token, *outs)


def on_device(images, texts, pairs, log_temp, bias):
    x_rows = images[0]
    y_rows = texts[0]
    rows = x_rows.shape[0]
    half = rows // 2
    size = lax.axis_size("dp")
    replicas = lax.axis_size("replica")
    numbers = jnp.concatenate([jnp.exp(log_temp), bias])
    core = lax.axis_index("replica") % 2
    swapped = core == 1
    moving_images = jnp.where(swapped, 1, 0).astype(jnp.int32).reshape(1)

    def send(value, to):
        return lax.ppermute(value, AXES, routes(size, replicas, to))

    def onward(value):
        return send(value, lambda z, c, k: (z + ahead(k), c))

    def back(value):
        return send(value, lambda z, c, k: (z - ahead(k), c))

    def across(value):
        return send(value, lambda z, c, k: (z, 1 - c))

    visits = [jnp.where(swapped, x_rows, y_rows)]
    held_b = jnp.where(swapped, y_rows[half:], x_rows[half:])
    held_a = jnp.where(swapped, y_rows[:half], x_rows[:half])
    held = jnp.concatenate([held_a, held_b], axis=0)
    for hop in range(3):
        visits.append(onward(visits[-1]))

    own = pairs[0]
    index = jnp.arange(rows, dtype=jnp.int32)
    inverse = jnp.sum(jnp.where(own == index[:, None], index[None, :], 0), axis=1)
    partner = jnp.where(swapped, inverse[None, :], own)

    sums = jnp.zeros((3, rows), jnp.float32)
    partial = {}
    gathered = {}
    residents = [held, None]
    for step, (which, hops) in enumerate(ORDER):
        if step == 1:
            next_a = send(across(held_a), lambda z, c, k: (z - ahead(k) * (c != k), c))
            next_b = send(held_b, lambda z, c, k: (z - ahead(k) * (c == k), c))
            next_b = across(next_b)
            residents[1] = jnp.concatenate([next_a, next_b], axis=0)
        last = step == len(ORDER) - 1
        outs, terms, sums = unit(
            step == 0,
            last,
            numbers,
            partner,
            sums,
            [visits[hop] for hop in hops],
            [residents[n] for n in which],
            [partial[hop] for hop in hops if hop in partial],
            [gathered[n] for n in which if n in gathered],
        )
        if not last:
            gathered.update(zip(which, outs))
        partial.update(zip(hops, terms))

    (ret_b,) = rest(*outs, visits[3], [gathered[1]], [(rows + half, half, half)])
    grad_own, ret_a = rest(
        *outs, hold(visits[3], ret_b), [gathered[0], gathered[1]], [(0, 0, rows), (rows, 0, half)]
    )

    stats = jnp.sum(sums, axis=1)

    def gather(bits, stats):
        for bit in bits:
            stats = exchange(stats, bit, size * replicas)
        return stats

    bits = [1 << n for n in range((size * replicas).bit_length() - 1)]
    column = [replicas // 2, replicas]
    levels = [bit for bit in bits if bit > replicas]
    inner = [bit for bit in bits if bit < replicas // 2]
    over_b = across(ret_b)
    stats = gather(inner + levels[:1], stats)
    total = add(back(partial[3]), partial[2], stats, over_b)
    up_a = send(hold(ret_a, total), lambda z, c, k: (z + ahead(k) * (c != k), c))
    home_b = send(hold(over_b, total), lambda z, c, k: (z + ahead(k) * (c == k), c))
    stats = gather(column + levels[1:2], stats)
    total = add(back(total), partial[1], stats, up_a, home_b)
    home_a = across(hold(up_a, total))
    total = back(total)
    stats = gather(levels[2:], stats)
    held_images = 1 - moving_images
    outs = place(0, held_images, home_a, grad_own, numbers, rows)
    outs = place(half, held_images, home_b, grad_own, numbers, rows, outs)
    grad_y, grad_x = place(0, moving_images, total, partial[0], numbers, rows, outs)
    count = float(HOPS * rows * rows * size * replicas)
    stats = stats / count
    return (grad_x[None], grad_y[None], stats)


def solution(mesh):
    placed = (
        P("replica", "dp", None),
        P("replica", "dp", None),
        P("replica", "dp", None),
        P(),
        P(),
    )
    return jax.shard_map(
        on_device,
        mesh=mesh,
        in_specs=placed,
        out_specs=(P("replica", "dp", None), P("replica", "dp", None), P()),
        check_vma=False,
    )
```

```python
import functools

import jax
import jax.numpy as jnp
from jax import lax
from jax.experimental import pallas as pl
from jax.experimental.pallas import tpu as pltpu
from jax.sharding import PartitionSpec as P

HOPS = 8
AXES = ("dp", "replica")
COLS = 2
PARTS = 3
MIB = 1024 * 1024
FLOPS_PER_US = 1.15e9

WHOLE = pl.BlockSpec(memory_space=pltpu.VMEM)
ANYWHERE = pl.BlockSpec(memory_space=pl.ANY)
SCALARS = pl.BlockSpec(memory_space=pltpu.SMEM)


ORDER = (
    ((0,), (0,)),
    ((0,), (1,)),
    ((1,), (0, 1)),
    ((0, 1), (2,)),
    ((0, 1), (3,)),
)


def f32(*shape):
    return jax.ShapeDtypeStruct(shape, jnp.float32)


def cost(micros):
    return pl.CostEstimate(
        flops=int(micros * FLOPS_PER_US), bytes_accessed=1024, transcendentals=0
    )


def limits(size=12):
    return pltpu.CompilerParams(vmem_limit_bytes=size * MIB)


def routes(size, replicas, to):
    levels = size // COLS
    pairs = []
    for level in range(levels):
        for col in range(COLS):
            for rep in range(replicas):
                new_level, new_col = to(level, col, rep % 2)
                source = (level * COLS + col) * replicas + rep
                target = ((new_level % levels) * COLS + new_col) * replicas + rep
                pairs.append((source, target))
    return pairs


def ahead(core):
    return 1 - 2 * core


def exchange(value, bit, total):
    return value + lax.ppermute(value, AXES, [(i, i ^ bit) for i in range(total)])


def split(value):
    high = value.astype(jnp.bfloat16)
    low = (value - high.astype(jnp.float32)).astype(jnp.bfloat16)
    return high, low


def dot3(a, b, dims):
    (i,), (j,) = dims
    left = jnp.concatenate([a[0], a[0], a[1]], axis=i)
    right = jnp.concatenate([b[0], b[1], b[0]], axis=j)
    return lax.dot_general(left, right, (dims, ((), ())), preferred_element_type=jnp.float32)


def stack(values, axis=0):
    return jnp.concatenate(values, axis=axis) if len(values) > 1 else values[0]


def hold_kernel(value, token, out):
    del value, token, out


def hold(value, token):
    return pl.pallas_call(
        hold_kernel,
        out_shape=f32(*value.shape),
        in_specs=[ANYWHERE] * 2,
        out_specs=ANYWHERE,
        input_output_aliases={0: 0},
        compiler_params=limits(),
        cost_estimate=cost(0.05),
    )(value, token)


def unit_kernel(first, later, counts, numbers, partner, before, *refs):
    residents, hops, with_earlier, with_gathered, pieces = counts
    taken = 0

    def take(count):
        nonlocal taken
        taken += count
        return refs[taken - count : taken]

    held, blocks = take(residents), take(hops)
    earlier, gathered = take(with_earlier), take(with_gathered)
    outs, grads, (after,) = take(pieces), take(hops), take(1)
    scale, shift_b = numbers[0], numbers[1]
    rows = held[0].shape[0]
    held_parts = split(stack([ref[...] for ref in held]))
    coefs, parts = [], []
    for i in range(3):
        after[i : i + 1, :] = before[i : i + 1, :]
    for hop in range(hops):
        block_parts = split(blocks[hop][...])
        product = scale * dot3(block_parts, held_parts, ((1,), (1,)))
        scores = product + shift_b
        small = jnp.exp(-jnp.abs(scores))
        share = 1.0 / (1.0 + small)
        coef = jnp.where(scores >= 0, share, small * share)
        loss = jnp.maximum(scores, 0.0) + jnp.log1p(small)
        if first:
            here = lax.broadcasted_iota(jnp.int32, scores.shape, 0) == partner[...]
            coef = coef - here.astype(jnp.float32)
            loss = loss - jnp.where(here, scores, 0.0)
        for i, values in enumerate((loss, coef * product, coef)):
            column_sums = jnp.sum(values, axis=0, keepdims=True)
            for n in range(residents):
                after[i : i + 1, :] += column_sums[:, n * rows : (n + 1) * rows]
        coef_parts = split(scale * coef)
        total = dot3(coef_parts, held_parts, ((1,), (0,)))
        grads[hop][...] = earlier[hop][...] + total if with_earlier else total
        coefs.append(coef_parts)
        parts.append(block_parts)
    if later:
        for n in range(2):
            outs[n][...] = coefs[0][n]
        return
    total = dot3(
        tuple(stack([value[n] for value in coefs]) for n in range(2)),
        tuple(stack([value[n] for value in parts]) for n in range(2)),
        ((0,), (0,)),
    )
    for i, out in enumerate(outs):
        term = total[i * rows : (i + 1) * rows]
        out[...] = gathered[i][...] + term if with_gathered else term


def unit(first, later, numbers, partner, before, blocks, held, earlier, gathered):
    if later:
        count = sum(value.shape[0] for value in held)
        first_shapes = [jax.ShapeDtypeStruct((blocks[0].shape[0], count), jnp.bfloat16)] * 2
        gathered = []
    else:
        first_shapes = [f32(*value.shape) for value in held]
    operands = [partner, before, *held, *blocks, *earlier, *gathered]
    counts = (len(held), len(blocks), len(earlier), len(gathered), len(first_shapes))
    outs = pl.pallas_call(
        functools.partial(unit_kernel, first, later, counts),
        out_shape=first_shapes
        + [f32(*block.shape) for block in blocks]
        + [f32(*before.shape)],
        in_specs=[SCALARS] + [WHOLE] * len(operands),
        out_specs=[WHOLE] * (len(first_shapes) + len(blocks) + 1),
        compiler_params=limits(14 + 8 * (len(held) * len(blocks) - 1)),
        cost_estimate=cost(7.0 * len(held) * len(blocks)),
    )(numbers, *operands)
    return outs[: len(first_shapes)], outs[len(first_shapes) : -1], outs[-1]


def rest_kernel(pieces, high, low, block, *refs):
    block_parts = split(block[...])
    for (column, start, count), sofar, out in zip(pieces, refs[: len(pieces)], refs[len(pieces) :]):
        place = pl.ds(column, count)
        term = dot3((high[:, place], low[:, place]), block_parts, ((0,), (0,)))
        out[...] = sofar[start : start + count, :] + term


def rest(high, low, block, sofar, pieces):
    width = block.shape[1]
    return pl.pallas_call(
        functools.partial(rest_kernel, pieces),
        out_shape=[f32(count, width) for _, _, count in pieces],
        in_specs=[WHOLE] * (3 + len(pieces)),
        out_specs=[WHOLE] * len(pieces),
        compiler_params=limits(16),
        cost_estimate=cost(0.007 * sum(count for _, _, count in pieces)),
    )(high, low, block, *sofar)


def add_kernel(left, right, *refs):
    refs[-1][...] = left[...] + right[...]


def add(left, right, *tokens):
    return pl.pallas_call(
        add_kernel,
        out_shape=f32(*left.shape),
        in_specs=[WHOLE] * 2 + [ANYWHERE] * len(tokens),
        out_specs=WHOLE,
        compiler_params=limits(),
        cost_estimate=cost(0.3),
    )(left, right, *tokens)


def place_kernel(start, chosen, left, right, token, *refs):
    out_x, out_y, total, sem = refs[-4:]
    height = total.shape[0] // PARTS

    def copies(out, i):
        rows = pl.ds(i * height, height)
        return pltpu.make_async_copy(total.at[rows], out.at[pl.ds(start + i * height, height)], sem.at[i])

    for i in range(PARTS):
        rows = pl.ds(i * height, height)
        more = right[rows, :] if right.shape == total.shape else right[pl.ds(start + i * height, height), :]
        total[rows, :] = left[rows, :] + more

        @pl.when(chosen[0] == 0)
        def _():
            copies(out_x, i).start()

        @pl.when(chosen[0] != 0)
        def _():
            copies(out_y, i).start()

    for i in range(PARTS):

        @pl.when(chosen[0] == 0)
        def _():
            copies(out_x, i).wait()

        @pl.when(chosen[0] != 0)
        def _():
            copies(out_y, i).wait()


def place(start, chosen, left, right, token, rows, outs=()):
    part, width = left.shape
    return pl.pallas_call(
        functools.partial(place_kernel, start),
        out_shape=[f32(rows, width)] * 2,
        in_specs=[SCALARS, WHOLE, WHOLE, WHOLE] + [ANYWHERE] * len(outs),
        out_specs=[ANYWHERE] * 2,
        scratch_shapes=[pltpu.VMEM((part, width), jnp.float32), pltpu.SemaphoreType.DMA((PARTS,))],
        input_output_aliases={4: 0, 5: 1} if outs else {},
        compiler_params=limits(),
        cost_estimate=cost(1.0),
    )(chosen, left, right, token, *outs)


def on_device(images, texts, pairs, log_temp, bias):
    x_rows = images[0]
    y_rows = texts[0]
    rows = x_rows.shape[0]
    half = rows // 2
    size = lax.axis_size("dp")
    replicas = lax.axis_size("replica")
    numbers = jnp.concatenate([jnp.exp(log_temp), bias])
    core = lax.axis_index("replica") % 2
    swapped = core == 1
    moving_images = jnp.where(swapped, 1, 0).astype(jnp.int32).reshape(1)

    def send(value, to):
        return lax.ppermute(value, AXES, routes(size, replicas, to))

    def onward(value):
        return send(value, lambda z, c, k: (z + ahead(k), c))

    def back(value):
        return send(value, lambda z, c, k: (z - ahead(k), c))

    def across(value):
        return send(value, lambda z, c, k: (z, 1 - c))

    visits = [jnp.where(swapped, x_rows, y_rows)]
    held_b = jnp.where(swapped, y_rows[half:], x_rows[half:])
    held_a = jnp.where(swapped, y_rows[:half], x_rows[:half])
    held = jnp.concatenate([held_a, held_b], axis=0)
    for hop in range(3):
        visits.append(onward(visits[-1]))

    own = pairs[0]
    index = jnp.arange(rows, dtype=jnp.int32)
    inverse = jnp.sum(jnp.where(own == index[:, None], index[None, :], 0), axis=1)
    partner = jnp.where(swapped, inverse[None, :], own)

    sums = jnp.zeros((3, rows), jnp.float32)
    partial = {}
    gathered = {}
    residents = [held, None]
    for step, (which, hops) in enumerate(ORDER):
        if step == 2:
            next_a = send(across(held_a), lambda z, c, k: (z - ahead(k) * (c != k), c))
            next_b = send(held_b, lambda z, c, k: (z - ahead(k) * (c == k), c))
            next_b = across(next_b)
            residents[1] = jnp.concatenate([next_a, next_b], axis=0)
        last = step == len(ORDER) - 1
        outs, terms, sums = unit(
            step == 0,
            last,
            numbers,
            partner,
            sums,
            [visits[hop] for hop in hops],
            [residents[n] for n in which],
            [partial[hop] for hop in hops if hop in partial],
            [gathered[n] for n in which if n in gathered],
        )
        if not last:
            gathered.update(zip(which, outs))
        partial.update(zip(hops, terms))

    (ret_b,) = rest(*outs, visits[3], [gathered[1]], [(rows + half, half, half)])
    grad_own, ret_a = rest(
        *outs, hold(visits[3], ret_b), [gathered[0], gathered[1]], [(0, 0, rows), (rows, 0, half)]
    )

    stats = jnp.sum(sums, axis=1)

    def gather(bits, stats):
        for bit in bits:
            stats = exchange(stats, bit, size * replicas)
        return stats

    bits = [1 << n for n in range((size * replicas).bit_length() - 1)]
    column = [replicas // 2, replicas]
    levels = [bit for bit in bits if bit > replicas]
    inner = [bit for bit in bits if bit < replicas // 2]
    over_b = across(ret_b)
    stats = hold(gather(inner, stats), ret_a)
    stats = gather(levels[:1], stats)
    total = add(back(partial[3]), partial[2], stats, over_b)
    up_a = send(hold(ret_a, total), lambda z, c, k: (z + ahead(k) * (c != k), c))
    home_b = send(hold(over_b, total), lambda z, c, k: (z + ahead(k) * (c == k), c))
    stats = gather(column + levels[1:2], stats)
    total = add(back(total), partial[1], stats, up_a, home_b)
    home_a = across(hold(up_a, total))
    total = back(total)
    stats = gather(levels[2:], stats)
    held_images = 1 - moving_images
    outs = place(half, held_images, home_b, grad_own, numbers, rows)
    outs = place(0, held_images, home_a, grad_own, numbers, rows, outs)
    grad_y, grad_x = place(0, moving_images, total, partial[0], numbers, rows, outs)
    count = float(HOPS * rows * rows * size * replicas)
    stats = stats / count
    return (grad_x[None], grad_y[None], stats)


def solution(mesh):
    placed = (
        P("replica", "dp", None),
        P("replica", "dp", None),
        P("replica", "dp", None),
        P(),
        P(),
    )
    return jax.shard_map(
        on_device,
        mesh=mesh,
        in_specs=placed,
        out_specs=(P("replica", "dp", None), P("replica", "dp", None), P()),
        check_vma=False,
    )
```

```python
import functools

import jax
import jax.numpy as jnp
from jax import lax
from jax.experimental import pallas as pl
from jax.experimental.pallas import tpu as pltpu
from jax.sharding import PartitionSpec as P

HOPS = 8
AXES = ("dp", "replica")
COLS = 2
PARTS = 3
MIB = 1024 * 1024
FLOPS_PER_US = 1.15e9

WHOLE = pl.BlockSpec(memory_space=pltpu.VMEM)
ANYWHERE = pl.BlockSpec(memory_space=pl.ANY)
SCALARS = pl.BlockSpec(memory_space=pltpu.SMEM)


ORDER = (
    ((0,), (0,)),
    ((0,), (1,)),
    ((1,), (0, 1)),
    ((0, 1), (2,)),
    ((0, 1), (3,)),
)


def f32(*shape):
    return jax.ShapeDtypeStruct(shape, jnp.float32)


def cost(micros):
    return pl.CostEstimate(
        flops=int(micros * FLOPS_PER_US), bytes_accessed=1024, transcendentals=0
    )


def limits(size=12):
    return pltpu.CompilerParams(vmem_limit_bytes=size * MIB)


def routes(size, replicas, to):
    levels = size // COLS
    pairs = []
    for level in range(levels):
        for col in range(COLS):
            for rep in range(replicas):
                new_level, new_col = to(level, col, rep % 2)
                source = (level * COLS + col) * replicas + rep
                target = ((new_level % levels) * COLS + new_col) * replicas + rep
                pairs.append((source, target))
    return pairs


def ahead(core):
    return 1 - 2 * core


def exchange(value, bit, total):
    return value + lax.ppermute(value, AXES, [(i, i ^ bit) for i in range(total)])


def split(value):
    high = value.astype(jnp.bfloat16)
    low = (value - high.astype(jnp.float32)).astype(jnp.bfloat16)
    return high, low


def dot3(a, b, dims):
    (i,), (j,) = dims
    left = jnp.concatenate([a[0], a[0], a[1]], axis=i)
    right = jnp.concatenate([b[0], b[1], b[0]], axis=j)
    return lax.dot_general(left, right, (dims, ((), ())), preferred_element_type=jnp.float32)


def stack(values, axis=0):
    return jnp.concatenate(values, axis=axis) if len(values) > 1 else values[0]


def hold_kernel(value, token, out):
    del value, token, out


def hold(value, token):
    return pl.pallas_call(
        hold_kernel,
        out_shape=f32(*value.shape),
        in_specs=[ANYWHERE] * 2,
        out_specs=ANYWHERE,
        input_output_aliases={0: 0},
        compiler_params=limits(),
        cost_estimate=cost(0.05),
    )(value, token)


def unit_kernel(first, later, counts, numbers, partner, before, *refs):
    residents, hops, with_earlier, with_gathered, pieces = counts
    taken = 0

    def take(count):
        nonlocal taken
        taken += count
        return refs[taken - count : taken]

    held, blocks = take(residents), take(hops)
    earlier, gathered = take(with_earlier), take(with_gathered)
    outs, grads, (after,) = take(pieces), take(hops), take(1)
    scale, shift_b = numbers[0], numbers[1]
    rows = held[0].shape[0]
    held_parts = split(stack([ref[...] for ref in held]))
    coefs, parts = [], []
    for i in range(3):
        after[i : i + 1, :] = before[i : i + 1, :]
    for hop in range(hops):
        block_parts = split(blocks[hop][...])
        product = scale * dot3(block_parts, held_parts, ((1,), (1,)))
        scores = product + shift_b
        small = jnp.exp(-jnp.abs(scores))
        share = 1.0 / (1.0 + small)
        coef = jnp.where(scores >= 0, share, small * share)
        loss = jnp.maximum(scores, 0.0) + jnp.log1p(small)
        if first:
            here = lax.broadcasted_iota(jnp.int32, scores.shape, 0) == partner[...]
            coef = coef - here.astype(jnp.float32)
            loss = loss - jnp.where(here, scores, 0.0)
        for i, values in enumerate((loss, coef * product, coef)):
            column_sums = jnp.sum(values, axis=0, keepdims=True)
            for n in range(residents):
                after[i : i + 1, :] += column_sums[:, n * rows : (n + 1) * rows]
        coef_parts = split(scale * coef)
        total = dot3(coef_parts, held_parts, ((1,), (0,)))
        grads[hop][...] = earlier[hop][...] + total if with_earlier else total
        coefs.append(coef_parts)
        parts.append(block_parts)
    if later:
        for n in range(2):
            outs[n][...] = coefs[0][n]
        return
    total = dot3(
        tuple(stack([value[n] for value in coefs]) for n in range(2)),
        tuple(stack([value[n] for value in parts]) for n in range(2)),
        ((0,), (0,)),
    )
    for i, out in enumerate(outs):
        term = total[i * rows : (i + 1) * rows]
        out[...] = gathered[i][...] + term if with_gathered else term


def unit(first, later, numbers, partner, before, blocks, held, earlier, gathered):
    if later:
        count = sum(value.shape[0] for value in held)
        first_shapes = [jax.ShapeDtypeStruct((blocks[0].shape[0], count), jnp.bfloat16)] * 2
        gathered = []
    else:
        first_shapes = [f32(*value.shape) for value in held]
    operands = [partner, before, *held, *blocks, *earlier, *gathered]
    counts = (len(held), len(blocks), len(earlier), len(gathered), len(first_shapes))
    outs = pl.pallas_call(
        functools.partial(unit_kernel, first, later, counts),
        out_shape=first_shapes
        + [f32(*block.shape) for block in blocks]
        + [f32(*before.shape)],
        in_specs=[SCALARS] + [WHOLE] * len(operands),
        out_specs=[WHOLE] * (len(first_shapes) + len(blocks) + 1),
        compiler_params=limits(14 + 8 * (len(held) * len(blocks) - 1)),
        cost_estimate=cost(7.0 * len(held) * len(blocks)),
    )(numbers, *operands)
    return outs[: len(first_shapes)], outs[len(first_shapes) : -1], outs[-1]


def rest_kernel(pieces, high, low, block, *refs):
    block_parts = split(block[...])
    for (column, start, count), sofar, out in zip(pieces, refs[: len(pieces)], refs[len(pieces) :]):
        place = pl.ds(column, count)
        term = dot3((high[:, place], low[:, place]), block_parts, ((0,), (0,)))
        out[...] = sofar[start : start + count, :] + term


def rest(high, low, block, sofar, pieces):
    width = block.shape[1]
    return pl.pallas_call(
        functools.partial(rest_kernel, pieces),
        out_shape=[f32(count, width) for _, _, count in pieces],
        in_specs=[WHOLE] * (3 + len(pieces)),
        out_specs=[WHOLE] * len(pieces),
        compiler_params=limits(16),
        cost_estimate=cost(0.007 * sum(count for _, _, count in pieces)),
    )(high, low, block, *sofar)


def add_kernel(left, right, *refs):
    refs[-1][...] = left[...] + right[...]


def add(left, right, *tokens):
    return pl.pallas_call(
        add_kernel,
        out_shape=f32(*left.shape),
        in_specs=[WHOLE] * 2 + [ANYWHERE] * len(tokens),
        out_specs=WHOLE,
        compiler_params=limits(),
        cost_estimate=cost(0.3),
    )(left, right, *tokens)


def place_kernel(start, chosen, left, right, token, *refs):
    out_x, out_y, total, sem = refs[-4:]
    height = total.shape[0] // PARTS

    def copies(out, i):
        rows = pl.ds(i * height, height)
        return pltpu.make_async_copy(total.at[rows], out.at[pl.ds(start + i * height, height)], sem.at[i])

    for i in range(PARTS):
        rows = pl.ds(i * height, height)
        more = right[rows, :] if right.shape == total.shape else right[pl.ds(start + i * height, height), :]
        total[rows, :] = left[rows, :] + more

        @pl.when(chosen[0] == 0)
        def _():
            copies(out_x, i).start()

        @pl.when(chosen[0] != 0)
        def _():
            copies(out_y, i).start()

    for i in range(PARTS):

        @pl.when(chosen[0] == 0)
        def _():
            copies(out_x, i).wait()

        @pl.when(chosen[0] != 0)
        def _():
            copies(out_y, i).wait()


def place(start, chosen, left, right, token, rows, outs=()):
    part, width = left.shape
    return pl.pallas_call(
        functools.partial(place_kernel, start),
        out_shape=[f32(rows, width)] * 2,
        in_specs=[SCALARS, WHOLE, WHOLE, WHOLE] + [ANYWHERE] * len(outs),
        out_specs=[ANYWHERE] * 2,
        scratch_shapes=[pltpu.VMEM((part, width), jnp.float32), pltpu.SemaphoreType.DMA((PARTS,))],
        input_output_aliases={4: 0, 5: 1} if outs else {},
        compiler_params=limits(),
        cost_estimate=cost(1.0),
    )(chosen, left, right, token, *outs)


def on_device(images, texts, pairs, log_temp, bias):
    x_rows = images[0]
    y_rows = texts[0]
    rows = x_rows.shape[0]
    half = rows // 2
    size = lax.axis_size("dp")
    replicas = lax.axis_size("replica")
    numbers = jnp.concatenate([jnp.exp(log_temp), bias])
    core = lax.axis_index("replica") % 2
    swapped = core == 1
    moving_images = jnp.where(swapped, 1, 0).astype(jnp.int32).reshape(1)

    def send(value, to):
        return lax.ppermute(value, AXES, routes(size, replicas, to))

    def onward(value):
        return send(value, lambda z, c, k: (z + ahead(k), c))

    def back(value):
        return send(value, lambda z, c, k: (z - ahead(k), c))

    def across(value):
        return send(value, lambda z, c, k: (z, 1 - c))

    visits = [jnp.where(swapped, x_rows, y_rows)]
    held_b = jnp.where(swapped, y_rows[half:], x_rows[half:])
    held_a = jnp.where(swapped, y_rows[:half], x_rows[:half])
    held = jnp.concatenate([held_a, held_b], axis=0)
    for hop in range(3):
        visits.append(onward(visits[-1]))

    own = pairs[0]
    index = jnp.arange(rows, dtype=jnp.int32)
    inverse = jnp.sum(jnp.where(own == index[:, None], index[None, :], 0), axis=1)
    partner = jnp.where(swapped, inverse[None, :], own)

    sums = jnp.zeros((3, rows), jnp.float32)
    partial = {}
    gathered = {}
    residents = [held, None]
    for step, (which, hops) in enumerate(ORDER):
        if step == 2:
            next_a = send(across(held_a), lambda z, c, k: (z - ahead(k) * (c != k), c))
            next_b = send(held_b, lambda z, c, k: (z - ahead(k) * (c == k), c))
            next_b = across(next_b)
            residents[1] = jnp.concatenate([next_a, next_b], axis=0)
        last = step == len(ORDER) - 1
        outs, terms, sums = unit(
            step == 0,
            last,
            numbers,
            partner,
            sums,
            [visits[hop] for hop in hops],
            [residents[n] for n in which],
            [partial[hop] for hop in hops if hop in partial],
            [gathered[n] for n in which if n in gathered],
        )
        if not last:
            gathered.update(zip(which, outs))
        partial.update(zip(hops, terms))

    (ret_b,) = rest(*outs, visits[3], [gathered[1]], [(rows + half, half, half)])
    own_a, own_b, ret_a = rest(
        *outs,
        hold(visits[3], ret_b),
        [gathered[0], gathered[0], gathered[1]],
        [(0, 0, half), (half, half, half), (rows, 0, half)],
    )

    stats = jnp.sum(sums, axis=1)

    def gather(bits, stats):
        for bit in bits:
            stats = exchange(stats, bit, size * replicas)
        return stats

    bits = [1 << n for n in range((size * replicas).bit_length() - 1)]
    column = [replicas // 2, replicas]
    levels = [bit for bit in bits if bit > replicas]
    inner = [bit for bit in bits if bit < replicas // 2]
    over_b = across(ret_b)
    stats = hold(gather(inner, stats), ret_a)
    stats = gather(levels[:1], stats)
    total = add(back(partial[3]), partial[2], stats, over_b)
    up_a = send(hold(ret_a, total), lambda z, c, k: (z + ahead(k) * (c != k), c))
    home_b = send(hold(over_b, total), lambda z, c, k: (z + ahead(k) * (c == k), c))
    stats = gather(column + levels[1:2], stats)
    total = add(back(total), partial[1], stats, up_a, home_b)
    home_a = across(hold(up_a, total))
    total = back(total)
    stats = gather(levels[2:], stats)
    held_images = 1 - moving_images
    outs = place(half, held_images, home_b, own_b, numbers, rows)
    outs = place(0, held_images, home_a, own_a, numbers, rows, outs)
    grad_y, grad_x = place(0, moving_images, total, partial[0], numbers, rows, outs)
    count = float(HOPS * rows * rows * size * replicas)
    stats = stats / count
    return (grad_x[None], grad_y[None], stats)


def solution(mesh):
    placed = (
        P("replica", "dp", None),
        P("replica", "dp", None),
        P("replica", "dp", None),
        P(),
        P(),
    )
    return jax.shard_map(
        on_device,
        mesh=mesh,
        in_specs=placed,
        out_specs=(P("replica", "dp", None), P("replica", "dp", None), P()),
        check_vma=False,
    )
```
